128 devices in a mesh: row: 8 (over x, z_hi), col: 16 (over y, z_lo, core).
Axes of the slice: x: 4, y: 4, z: 4 (z_hi: 2, z_lo: 2; z = z_hi * 2 + z_lo), core: 2. Of those that a mesh axis runs over, the one named last changes fastest.
Arguments:
- features: bfloat16 [65536, 128], P(('col', 'row')), may hold values from -6 to 6
- weight: bfloat16 [128, 256], replicated, may hold values from -0.5 to 0.5
- bias: float32 [256], replicated, may hold values from -3 to 3
- tile_values: bfloat16 [8, 16, 704, 128, 128], P('row', 'col'), may hold values from -0.0390625 to 0.0390625
- tile_rows: int32 [8, 16, 704], P('row', 'col'), may hold values from 0 to 63
- tile_cols: int32 [8, 16, 704], P('row', 'col'), may hold values from 0 to 31
- tile_count: int32 [8, 16], P('row', 'col'), may hold values from 88 to 704, as said below
- upstream: bfloat16 [65536, 256], P(('row', 'col')), may hold values from -6 to 6
Outputs:
- activated: bfloat16 [65536, 256], P(('row', 'col'))
- feature_grad: bfloat16 [65536, 128], P(('col', 'row'))
- weight_grad: float32 [128, 256], replicated
- bias_grad: float32 [256], replicated
The draws below stay inside these ranges and needn't reach their ends.
Inputs may be any that keep to these rules, and one draw needn't show every extreme that they name: Each device uses only its first tile_count slots; some devices use all 704.
All inputs are finite; a program needn't handle non-finite values.
Results may differ from the reference program's by a relative error of at most 0.0075.
Values may be sent and summed in bfloat16 or wider, within the bound.
No kernel may reach another device: no remote copies, remote signals or barrier semaphores. Data moves between devices by JAX's collectives and lax.ppermute only.
A program may use at most 256 MiB of HBM per device.

```python
import jax
import jax.numpy as jnp
from jax import lax

F_IN = 128
HID = 256
TILE = 128
NODES_DEV = 512
TILES_DEV = 704
NODES = 65536
ROW_TILES = 64
COL_TILES = 32
N_ROW = 8
N_COL = 16


def draw_tile_count(key, part):
    key = jax.random.fold_in(key, 7)
    index_row = jnp.arange(N_ROW, dtype=jnp.int32)[:, None]
    index_col = jnp.arange(N_COL, dtype=jnp.int32)[None, :]
    band = (index_row * N_COL < (index_col + 1) * N_ROW) & (index_col * N_ROW < (index_row + 1) * N_COL)
    lowest = max(1, TILES_DEV // 8)
    highest = max(lowest + 1, TILES_DEV)
    drawn = jax.random.randint(key, (N_ROW, N_COL), lowest, highest, dtype=jnp.int32)
    return jnp.where(band, TILES_DEV, drawn).astype(jnp.int32)


def set_ends(result, rng, low, largest):
    dims = result.shape
    spot = [jax.random.randint(jax.random.fold_in(rng, axis), (), 0, dims[axis]) for axis in range(len(dims))]
    result = result.at[tuple(spot)].set(low)
    longest = dims.index(max(dims))
    spot[longest] = (spot[longest] + 1) % dims[longest]
    return result.at[tuple(spot)].set(largest)


def level_of(rng, shape, pieces, least, high):
    def one(position, shards_of):
        heights = jax.random.uniform(jax.random.fold_in(jax.random.fold_in(rng, 6), position), (shards_of,), jnp.float32, least / len(pieces), high / len(pieces))
        return jnp.repeat(jnp.exp(heights), shape[position] // shards_of).reshape((-1,) + (1,) * (len(shape) - position - 1))

    factor_of = one(*pieces[0])
    for cut in pieces[1:]:
        factor_of = factor_of * one(*cut)
    return factor_of


def bell_draw(rng, dims, width, reach, cuts=(), kind=jnp.bfloat16):
    array = jax.random.normal(rng, dims, jnp.float32) * width
    if len(cuts) > 0:
        array = level_of(rng, dims, cuts, -0.22, 0.18) * array
    return jnp.clip(array, min=-reach, max=reach).astype(kind)


def setup_inputs(seed: int = 0) -> dict:
    seeds = jax.random.split(jax.random.key(seed), 9)
    return {
        "features": bell_draw(seeds[0], (NODES, F_IN), 1.0, 6.0, ((0, 128),)),
        "weight": bell_draw(seeds[1], (F_IN, HID), F_IN ** -0.5, 0.5),
        "bias": bell_draw(seeds[2], (HID,), 0.5, 3.0, (), jnp.float32),
        "tile_values": bell_draw(seeds[3], (N_ROW, N_COL, TILES_DEV, TILE, TILE), (TILES_DEV * TILE * TILE // NODES_DEV) ** -0.5, 0.0390625, ((0, 8), (1, 16))),
        "tile_rows": set_ends(jax.random.randint(seeds[4], (N_ROW, N_COL, TILES_DEV), 0, ROW_TILES), jax.random.fold_in(seeds[4], 1), 0, ROW_TILES - 1).astype(jnp.int32),
        "tile_cols": set_ends(jax.random.randint(seeds[5], (N_ROW, N_COL, TILES_DEV), 0, COL_TILES), jax.random.fold_in(seeds[5], 1), 0, COL_TILES - 1).astype(jnp.int32),
        "tile_count": draw_tile_count(jax.random.fold_in(seeds[8], 71), 0),
        "upstream": bell_draw(seeds[7], (NODES, HID), 1.0, 6.0, ((0, 128),)),
    }


def tile_apply(values, rows, cols, count, source, num_out, transposed):
    slots = jnp.arange(values.shape[0], dtype=jnp.int32)
    live = slots < count
    if transposed:
        picked = source[rows]
        prod = jnp.einsum('tba,tbf->taf', values.astype(jnp.float32), picked.astype(jnp.float32))
        target = jnp.where(live, cols, num_out)
    else:
        picked = source[cols]
        prod = jnp.einsum('tab,tbf->taf', values.astype(jnp.float32), picked.astype(jnp.float32))
        target = jnp.where(live, rows, num_out)
    summed = jax.ops.segment_sum(prod, target, num_segments=num_out + 1)
    return summed[:num_out]

def reference(features, weight, bias, tile_values, tile_rows, tile_cols, tile_count, upstream):
    col_blocks = features.reshape(N_COL, COL_TILES, TILE, F_IN)

    def forward_row(i):

        def step(total, j):
            part = tile_apply(tile_values[i, j], tile_rows[i, j], tile_cols[i, j], tile_count[i, j], col_blocks[j], ROW_TILES, False)
            return (total + part, None)
        start = jnp.zeros((ROW_TILES, TILE, F_IN), jnp.float32)
        total, unused = lax.scan(step, start, jnp.arange(N_COL, dtype=jnp.int32))
        return total
    aggregated = lax.map(forward_row, jnp.arange(N_ROW, dtype=jnp.int32))
    s_half = aggregated.reshape(NODES, F_IN).astype(jnp.bfloat16)
    pre = jnp.dot(s_half, weight, preferred_element_type=jnp.float32) + bias
    activated = jax.nn.gelu(pre, approximate=True).astype(jnp.bfloat16)
    unused_out, pullback = jax.vjp(lambda v: jax.nn.gelu(v, approximate=True), pre)
    grad_pre = pullback(upstream.astype(jnp.float32))[0].astype(jnp.bfloat16)
    weight_grad = jnp.dot(s_half.T, grad_pre, preferred_element_type=jnp.float32)
    bias_grad = lax.optimization_barrier(jnp.sum(grad_pre.astype(jnp.float32), axis=0))
    grad_agg = jnp.dot(grad_pre, weight.T, preferred_element_type=jnp.float32).astype(jnp.bfloat16)
    row_blocks = grad_agg.reshape(N_ROW, ROW_TILES, TILE, F_IN)

    def backward_col(j):

        def step(total, i):
            part = tile_apply(tile_values[i, j], tile_rows[i, j], tile_cols[i, j], tile_count[i, j], row_blocks[i], COL_TILES, True)
            return (total + part, None)
        start = jnp.zeros((COL_TILES, TILE, F_IN), jnp.float32)
        total, unused = lax.scan(step, start, jnp.arange(N_ROW, dtype=jnp.int32))
        return total
    feature_grad = lax.map(backward_col, jnp.arange(N_COL, dtype=jnp.int32))
    feature_grad = feature_grad.reshape(NODES, F_IN).astype(jnp.bfloat16)
    return (activated, feature_grad, weight_grad, bias_grad)
```

```python
import functools

import jax
import jax.numpy as jnp
from jax import lax
from jax.experimental import pallas as pl
from jax.experimental.pallas import tpu as pltpu
from jax.sharding import PartitionSpec as P

HALF = jnp.bfloat16
FULL = jnp.float32


def swap(array, axis, distance):
    size = lax.axis_size(axis)
    return lax.ppermute(array, axis, [(j, j ^ distance) for j in range(size)])


def tile_kernel(chunk, num_pieces, flip, live_ref, source_ref, target_ref, *refs):
    values_hbm = refs[0]
    pieces = refs[1 : 1 + num_pieces]
    outs = refs[1 + num_pieces : -4]
    source, values, total, sems = refs[-4:]
    num_chunks = values.shape[0] // chunk

    def copy(i):
        span = pl.ds(i * chunk, chunk)
        return pltpu.make_async_copy(values_hbm.at[span], values.at[span], sems.at[i])

    live_chunks = live_ref[0]
    for i in range(num_chunks):

        @pl.when(i < live_chunks)
        def _():
            copy(i).start()

    first = 0
    for piece in pieces:
        source[pl.ds(first, piece.shape[0])] = piece[...]
        first += piece.shape[0]
    total[...] = jnp.zeros_like(total)

    def step(i, carry):
        copy(i).wait()
        products = []
        for u in range(chunk):
            slot = i * chunk + u
            picked = source[source_ref[slot]]
            pair = (picked, values[slot]) if flip else (values[slot], picked)
            products.append(jnp.dot(*pair, preferred_element_type=FULL))
        for u in range(chunk):
            total[target_ref[i * chunk + u]] += products[u]
        return carry

    lax.fori_loop(0, live_chunks, step, 0)
    first = 0
    for out in outs:
        out[...] = total[pl.ds(first, out.shape[0])].astype(out.dtype)
        first += out.shape[0]


def tile_sums(values, pieces, source_index, target_index, count, out_types, flip):
    slots, side, _ = values.shape
    chunk = max(d for d in range(1, 65) if slots % d == 0)
    num_source = sum(piece.shape[0] for piece in pieces)
    num_out = sum(n for n, _ in out_types)
    width = pieces[0].shape[2]
    target_index = jnp.where(jnp.arange(slots, dtype=jnp.int32) < count, target_index, num_out)
    live_chunks = ((count + chunk - 1) // chunk).reshape(1)
    smem = pl.BlockSpec(memory_space=pltpu.SMEM)
    vmem = pl.BlockSpec(memory_space=pltpu.VMEM)
    return pl.pallas_call(
        functools.partial(tile_kernel, chunk, len(pieces), flip),
        out_shape=[jax.ShapeDtypeStruct((n, side, width), kind) for n, kind in out_types],
        in_specs=[smem] * 3 + [pl.BlockSpec(memory_space=pl.ANY)] + [vmem] * len(pieces),
        out_specs=[vmem] * len(out_types),
        scratch_shapes=[
            pltpu.VMEM((num_source, side, width), HALF),
            pltpu.VMEM((slots, side, side), HALF),
            pltpu.VMEM((num_out + 1, side, width), FULL),
            pltpu.SemaphoreType.DMA((slots // chunk,)),
        ],
        compiler_params=pltpu.CompilerParams(vmem_limit_bytes=42 * 2**20),
    )(live_chunks, source_index, target_index, values, *pieces)


def all_sum(array):
    half = array.shape[0] // 2
    low, high = array[:half], array[half:]
    odd = lax.axis_index("col") % 2 == 1
    array = jnp.where(odd, high, low) + swap(jnp.where(odd, low, high), "col", 1)
    array = array + swap(array, "col", 2)
    array = (array + swap(array, "col", 4)) + (swap(array, "col", 8) + swap(array, "col", 12))
    array = array + swap(array, "row", 1)
    array = (array + swap(array, "row", 2)) + (swap(array, "row", 4) + swap(array, "row", 6))
    other = swap(array, "col", 1)
    return jnp.concatenate([jnp.where(odd, other, array), jnp.where(odd, array, other)], axis=0)


def shards(features, weight, bias, tile_values, tile_rows, tile_cols, tile_count, upstream):
    side = tile_values.shape[3]
    width = features.shape[1]
    hidden = weight.shape[1]
    nodes = features.shape[0]
    per = nodes // side
    values = tile_values[0, 0]
    rows = tile_rows[0, 0]
    cols = tile_cols[0, 0]
    count = tile_count[0, 0]
    my_row = lax.axis_index("row")
    my_col = lax.axis_index("col")
    row_owner = (rows // per) ^ my_col
    row_place = (row_owner % 2) * (lax.axis_size("col") // 2 * per) + (row_owner // 2) * per + rows % per
    col_place = ((cols // per) ^ my_row) * per + cols % per

    own = features.reshape(per, side, width)
    pair = jnp.concatenate([own, swap(own, "row", 1)], axis=0)
    pieces = [pair] + [swap(pair, "row", d) for d in (2, 4, 6)]
    half_tiles = lax.axis_size("col") // 2 * per
    keep, send = tile_sums(
        values, pieces, col_place, row_place, count, [(half_tiles, FULL), (half_tiles, HALF)], False
    )

    block = (keep + swap(send, "col", 1).astype(FULL)).astype(HALF).reshape(4, 2 * per, side, width)
    total = block[0].astype(FULL)
    for other in [swap(block[d], "col", 4 * d) for d in (1, 2, 3)]:
        total = total + other.astype(FULL)
    away = swap(total[per:].astype(HALF), "col", 2)
    s_half = (total[:per] + away.astype(FULL)).astype(HALF).reshape(nodes, width)

    pre = jnp.dot(s_half, weight, preferred_element_type=FULL) + bias
    activated = jax.nn.gelu(pre, approximate=True).astype(HALF)
    _, pullback = jax.vjp(lambda v: jax.nn.gelu(v, approximate=True), pre)
    grad_pre = pullback(upstream.astype(FULL))[0].astype(HALF)
    grad_tiles = grad_pre.reshape(per, side, hidden)
    grad_agg = jnp.einsum("fh,tbh->tfb", weight, grad_tiles, preferred_element_type=FULL).astype(HALF)

    pair = jnp.concatenate([grad_agg, swap(grad_agg, "col", 2)], axis=0)
    near = [pair] + [swap(pair, "col", d) for d in (4, 8, 12)]
    far = [swap(piece, "col", 1) for piece in near]
    (back,) = tile_sums(
        values, near + far, row_place, col_place, count, [(lax.axis_size("row") * per, HALF)], True
    )

    weight_term = jnp.dot(s_half.T, grad_pre, preferred_element_type=FULL)
    bias_term = jnp.sum(grad_pre.astype(FULL), axis=0)
    terms = jnp.concatenate([weight_term, jnp.broadcast_to(bias_term[None], (16, hidden))], axis=0)
    terms = all_sum(terms)
    weight_grad, bias_grad = terms[:width], terms[width]

    back = back.reshape(4, 2 * per, side, side)
    total = back[0].astype(FULL)
    for other in [swap(back[d], "row", 2 * d) for d in (1, 2, 3)]:
        total = total + other.astype(FULL)
    away = swap(total[per:].astype(HALF), "row", 1)
    total = total[:per] + away.astype(FULL)
    feature_grad = jnp.swapaxes(total, 1, 2).astype(HALF).reshape(nodes, width)
    return (activated, feature_grad, weight_grad, bias_grad)


def solution(mesh):
    in_specs = (
        P(("col", "row"), None),
        P(),
        P(),
        P("row", "col", None, None, None),
        P("row", "col", None),
        P("row", "col", None),
        P("row", "col"),
        P(("row", "col"), None),
    )
    out_specs = (P(("row", "col"), None), P(("col", "row"), None), P(), P())
    return jax.shard_map(shards, mesh=mesh, in_specs=in_specs, out_specs=out_specs, check_vma=False)
```

```python
import functools

import jax
import jax.numpy as jnp
from jax import lax
from jax.experimental import pallas as pl
from jax.experimental.pallas import tpu as pltpu
from jax.sharding import PartitionSpec as P

HALF = jnp.bfloat16
FULL = jnp.float32


def swap(array, axis, distance):
    size = lax.axis_size(axis)
    return lax.ppermute(array, axis, [(j, j ^ distance) for j in range(size)])


def tile_kernel(chunk, num_pieces, flip, table_ref, *refs):
    values_hbm = refs[0]
    pieces = refs[1 : 1 + num_pieces]
    *outs, done = refs[1 + num_pieces : -4]
    source, values, total, sems = refs[-4:]
    num_chunks = values.shape[0] // chunk

    def copy(i):
        span = pl.ds(i * chunk, chunk)
        return pltpu.make_async_copy(values_hbm.at[span], values.at[span], sems.at[i])

    live_chunks = table_ref[values.shape[0]]
    for i in range(num_chunks):

        @pl.when(i < live_chunks)
        def _():
            copy(i).start()

    first = 0
    for piece in pieces:
        tiles = piece.shape[0] // source.shape[1]
        source[pl.ds(first, tiles)] = piece[...].reshape((tiles,) + source.shape[1:])
        first += tiles
    total[...] = jnp.zeros_like(total)

    def step(i, carry):
        copy(i).wait()
        products, targets = [], []
        for u in range(chunk):
            slot = i * chunk + u
            entry = table_ref[slot]
            picked = source[entry & 255]
            pair = (picked, values[slot]) if flip else (values[slot], picked)
            products.append(jnp.dot(*pair, preferred_element_type=FULL))
            targets.append(entry >> 8)
        for target, product in zip(targets, products):
            total[target] += product
        return carry

    lax.fori_loop(0, live_chunks, step, 0)
    first = 0
    for out in outs:
        tiles = out.shape[0] // total.shape[1]
        out[...] = total[pl.ds(first, tiles)].astype(out.dtype).reshape(out.shape)
        first += tiles
    done[...] = jnp.zeros_like(done)


def tile_sums(values, pieces, source_index, target_index, count, out_types, flip, zero_shape=(8, 128)):
    slots, side, _ = values.shape
    chunk = max(d for d in range(1, 65) if slots % d == 0)
    num_source = sum(piece.shape[0] for piece in pieces) // side
    num_out = sum(n for n, _ in out_types)
    width = pieces[0].shape[1]
    target_index = jnp.where(jnp.arange(slots, dtype=jnp.int32) < count, target_index, num_out)
    table = jnp.concatenate([source_index | (target_index << 8), (count + chunk - 1) // chunk])
    smem = pl.BlockSpec(memory_space=pltpu.SMEM)
    vmem = pl.BlockSpec(memory_space=pltpu.VMEM)
    return pl.pallas_call(
        functools.partial(tile_kernel, chunk, len(pieces), flip),
        out_shape=[jax.ShapeDtypeStruct((n * side, width), kind) for n, kind in out_types]
        + [jax.ShapeDtypeStruct(zero_shape, FULL)],
        in_specs=[smem, pl.BlockSpec(memory_space=pltpu.HBM)] + [vmem] * len(pieces),
        out_specs=[vmem] * (len(out_types) + 1),
        scratch_shapes=[
            pltpu.VMEM((num_source, side, width), HALF),
            pltpu.VMEM((slots, side, side), HALF),
            pltpu.VMEM((num_out + 1, side, width), FULL),
            pltpu.SemaphoreType.DMA((slots // chunk,)),
        ],
        cost_estimate=pl.CostEstimate(
            flops=8 * slots * side * side * width, bytes_accessed=2 * slots * side * side, transcendentals=0
        ),
        compiler_params=pltpu.CompilerParams(vmem_limit_bytes=42 * 2**20),
    )(table, pltpu.with_memory_space_constraint(values, pltpu.HBM), *pieces)


def after(array, event):
    return lax.optimization_barrier((array, event))[0]


def shards(features, weight, bias, tile_values, tile_rows, tile_cols, tile_count, upstream):
    side = tile_values.shape[3]
    width = features.shape[1]
    hidden = weight.shape[1]
    nodes = features.shape[0]
    per = nodes // side
    values = tile_values.reshape(tile_values.shape[2:])
    rows = tile_rows.reshape(-1)
    cols = tile_cols.reshape(-1)
    count = tile_count.reshape(1)
    my_row = lax.axis_index("row")
    my_col = lax.axis_index("col")
    row_owner = (rows // per) ^ my_col
    row_place = (row_owner % 2) * (lax.axis_size("col") // 2 * per) + (row_owner // 2) * per + rows % per
    col_place = ((cols // per) ^ my_row) * per + cols % per

    pair = jnp.concatenate([features, swap(features, "row", 1)], axis=0)
    pieces = [pair] + [swap(pair, "row", d) for d in (2, 4, 6)]
    half_tiles = lax.axis_size("col") // 2 * per
    keep, send, _ = tile_sums(
        values, pieces, col_place, row_place, count, [(half_tiles, FULL), (half_tiles, HALF)], False
    )

    block = (keep + swap(send, "col", 1).astype(FULL)).astype(HALF).reshape(4, 2 * nodes, width)
    total = block[0].astype(FULL)
    for other in [swap(block[d], "col", 4 * d) for d in (2, 1, 3)]:
        total = total + other.astype(FULL)
    away = swap(total[nodes:].astype(HALF), "col", 2)
    s_half = (total[:nodes] + away.astype(FULL)).astype(HALF)

    pre = jnp.dot(s_half, weight, preferred_element_type=FULL) + bias
    activated = jax.nn.gelu(pre, approximate=True).astype(HALF)
    _, pullback = jax.vjp(lambda v: jax.nn.gelu(v, approximate=True), pre)
    grad_pre = pullback(upstream.astype(FULL))[0].astype(HALF)
    grad_tiles = grad_pre.reshape(per, side, hidden)
    grad_agg = jnp.einsum("fh,tbh->tfb", weight, grad_tiles, preferred_element_type=FULL).astype(HALF)
    grad_agg = grad_agg.reshape(per * width, side)

    pair = jnp.concatenate([grad_agg, swap(grad_agg, "col", 2)], axis=0)
    s_half, grad_pre = after((s_half, grad_pre), grad_agg)
    weight_term = jnp.dot(s_half.T, grad_pre, preferred_element_type=FULL)
    bias_term = jnp.sum(grad_pre.astype(FULL), axis=0)
    terms = jnp.concatenate([weight_term, jnp.broadcast_to(bias_term[None], (8, hidden))], axis=0)
    terms = terms + swap(terms, "col", 1)
    near = [pair] + [swap(pair, "col", d) for d in (4, 8, 12)]
    terms = after(terms, pair)
    terms = (terms + swap(terms, "row", 2)) + (swap(terms, "row", 4) + swap(terms, "row", 6))
    far = [swap(piece, "col", 1) for piece in near]
    terms = after(terms, near)
    other_terms = swap(terms, "row", 1)
    back, zero = tile_sums(
        values, near + far, row_place, col_place, count, [(lax.axis_size("row") * per, HALF)], True, terms.shape
    )
    back = back.reshape(4, 2 * nodes, side)
    total = back[0].astype(FULL)
    for other in [swap(back[d], "row", 2 * d) for d in (2, 1, 3)]:
        total = total + other.astype(FULL)
    terms = (terms + zero) + other_terms
    terms = terms + swap(terms, "col", 2)
    terms = (terms + swap(terms, "col", 4)) + (swap(terms, "col", 8) + swap(terms, "col", 12))
    away = swap(total[nodes:].astype(HALF), "row", 1)
    total = total[:nodes] + away.astype(FULL)
    feature_grad = jnp.swapaxes(total.reshape(per, width, side), 1, 2).astype(HALF).reshape(nodes, width)
    return (activated, feature_grad, terms[:width], terms[width])


def solution(mesh):
    in_specs = (
        P(("col", "row"), None),
        P(),
        P(),
        P("row", "col", None, None, None),
        P("row", "col", None),
        P("row", "col", None),
        P("row", "col"),
        P(("row", "col"), None),
    )
    out_specs = (P(("row", "col"), None), P(("col", "row"), None), P(), P())
    return jax.shard_map(shards, mesh=mesh, in_specs=in_specs, out_specs=out_specs, check_vma=False)
```

```python
import functools

import jax
import jax.numpy as jnp
from jax import lax
from jax.experimental import pallas as pl
from jax.experimental.pallas import tpu as pltpu
from jax.sharding import PartitionSpec as P

HALF = jnp.bfloat16
FULL = jnp.float32


def swap(array, axis, distance):
    size = lax.axis_size(axis)
    return lax.ppermute(array, axis, [(j, j ^ distance) for j in range(size)])


def tile_kernel(chunk, num_pieces, num_totals, num_ready, flip, table_any, *refs):
    values_hbm = refs[0]
    pieces = refs[1 : 1 + num_pieces]
    outs = refs[1 + num_pieces + num_ready : -6]
    source, values, total, sems = refs[-6:-2]
    table_ref, table_sem = refs[-2:]
    num_chunks = values.shape[0] // chunk

    def copy(i):
        span = pl.ds(i * chunk, chunk)
        return pltpu.make_async_copy(values_hbm.at[span], values.at[span], sems.at[i])

    fetch = pltpu.make_async_copy(table_any, table_ref, table_sem)
    fetch.start()
    copy(0).start()
    first = 0
    for piece in pieces:
        tiles = piece.shape[0] // source.shape[1]
        source[pl.ds(first, tiles)] = piece[...].reshape((tiles,) + source.shape[1:])
        first += tiles
    fetch.wait()
    live_chunks = table_ref[values.shape[0]]
    for i in range(1, num_chunks):

        @pl.when(i < live_chunks)
        def _():
            copy(i).start()

    total[...] = jnp.zeros_like(total)

    def step(i, carry):
        copy(i).wait()
        products, targets = [], []
        for u in range(chunk):
            slot = i * chunk + u
            entry = table_ref[slot]
            picked = source[entry & 255]
            pair = (picked, values[slot]) if flip else (values[slot], picked)
            products.append(jnp.dot(*pair, preferred_element_type=FULL))
            targets.append(entry >> 8)
        for target, product in zip(targets, products):
            total[target] += product
        return carry

    lax.fori_loop(0, live_chunks, step, 0)
    first = 0
    for out in outs[:num_totals]:
        tiles = out.shape[0] // total.shape[1]
        out[...] = total[pl.ds(first, tiles)].astype(out.dtype).reshape(out.shape)
        first += tiles
    for out in outs[num_totals:]:
        out[...] = jnp.zeros_like(out)


def tile_sums(values, pieces, source_index, target_index, count, out_types, flip, zero_shape=None, ready=None):
    slots, side, _ = values.shape
    chunk = max(d for d in range(1, 65) if slots % d == 0)
    num_source = sum(piece.shape[0] for piece in pieces) // side
    num_out = sum(n for n, _ in out_types)
    width = pieces[0].shape[1]
    target_index = jnp.where(jnp.arange(slots, dtype=jnp.int32) < count, target_index, num_out)
    table = jnp.concatenate([source_index | (target_index << 8), jnp.maximum((count + chunk - 1) // chunk, 1)])
    vmem = pl.BlockSpec(memory_space=pltpu.VMEM)
    return pl.pallas_call(
        functools.partial(tile_kernel, chunk, len(pieces), len(out_types), int(ready is not None), flip),
        out_shape=[jax.ShapeDtypeStruct((n * side, width), kind) for n, kind in out_types]
        + ([jax.ShapeDtypeStruct(zero_shape, FULL)] if zero_shape else []),
        in_specs=[pl.BlockSpec(memory_space=pl.ANY), pl.BlockSpec(memory_space=pltpu.HBM)] + [vmem] * len(pieces)
        + [pl.BlockSpec(memory_space=pl.ANY)] * (ready is not None),
        out_specs=[vmem] * (len(out_types) + bool(zero_shape)),
        scratch_shapes=[
            pltpu.VMEM((num_source, side, width), HALF),
            pltpu.VMEM((slots, side, side), HALF),
            pltpu.VMEM((num_out + 1, side, width), FULL),
            pltpu.SemaphoreType.DMA((slots // chunk,)),
            pltpu.SMEM(table.shape, jnp.int32),
            pltpu.SemaphoreType.DMA,
        ],
        cost_estimate=pl.CostEstimate(
            flops=8 * slots * side * side * width, bytes_accessed=2 * slots * side * side, transcendentals=0
        ),
        compiler_params=pltpu.CompilerParams(vmem_limit_bytes=42 * 2**20),
    )(table, pltpu.with_memory_space_constraint(values, pltpu.HBM), *pieces, *([] if ready is None else [ready]))


def after(array, event):
    return lax.optimization_barrier((array, event))[0]


def shards(features, weight, bias, tile_values, tile_rows, tile_cols, tile_count, upstream):
    side = tile_values.shape[3]
    width = features.shape[1]
    hidden = weight.shape[1]
    nodes = features.shape[0]
    per = nodes // side
    values = tile_values.reshape(tile_values.shape[2:])
    rows = tile_rows.reshape(-1)
    cols = tile_cols.reshape(-1)
    count = tile_count.reshape(1)
    my_row = lax.axis_index("row")
    my_col = lax.axis_index("col")
    row_owner = (rows // per) ^ my_col
    row_place = (row_owner % 2) * (lax.axis_size("col") // 2 * per) + (row_owner // 2) * per + rows % per
    col_place = ((cols // per) ^ my_row) * per + cols % per

    pair = jnp.concatenate([features, swap(features, "row", 1)], axis=0)
    pieces = [pair] + [swap(pair, "row", d) for d in (2, 4, 6)]
    up_away = swap(upstream, "col", 2)
    half_tiles = lax.axis_size("col") // 2 * per
    keep, send = tile_sums(
        values, pieces, col_place, row_place, count, [(half_tiles, FULL), (half_tiles, HALF)], False, ready=up_away
    )

    block = (keep + swap(send, "col", 1).astype(FULL)).astype(HALF).reshape(4, 2 * nodes, width)
    total = block[0].astype(FULL)
    for other in [swap(block[d], "col", 4 * d) for d in (2, 1, 3)]:
        total = total + other.astype(FULL)
    both = total.astype(HALF)
    both = (both.astype(FULL) + swap(jnp.concatenate([both[nodes:], both[:nodes]], axis=0), "col", 2).astype(FULL)).astype(HALF)
    up = jnp.concatenate([upstream, up_away], axis=0)
    pre = jnp.dot(both, weight, preferred_element_type=FULL) + bias
    activated = jax.nn.gelu(pre[:nodes], approximate=True).astype(HALF)
    _, pullback = jax.vjp(lambda v: jax.nn.gelu(v, approximate=True), pre)
    grad_both = pullback(up.astype(FULL))[0].astype(HALF)
    grad_tiles = grad_both.reshape(2 * per, side, hidden)
    pair = jnp.einsum("fh,tbh->tfb", weight, grad_tiles, preferred_element_type=FULL).astype(HALF)
    pair = pair.reshape(2 * per * width, side)
    grad_agg = pair
    s_half, grad_pre = both[:nodes], grad_both[:nodes]

    s_half, grad_pre = after((s_half, grad_pre), grad_agg)
    weight_term = jnp.dot(s_half.T, grad_pre, preferred_element_type=FULL)
    bias_term = jnp.sum(grad_pre.astype(FULL), axis=0)
    terms = jnp.concatenate([weight_term, jnp.broadcast_to(bias_term[None], (8, hidden))], axis=0)
    terms = (terms + swap(terms, "row", 2)) + (swap(terms, "row", 4) + swap(terms, "row", 6))
    near = [pair] + [swap(pair, "col", d) for d in (4, 8, 12)]
    far = [swap(piece, "col", 1) for piece in near]
    other_terms = [swap(terms, "row", 1)]
    back, zero = tile_sums(
        values, near + far, row_place, col_place, count, [(lax.axis_size("row") * per, HALF)], True, terms.shape
    )
    back = back.reshape(4, 2 * nodes, side)
    total = back[0].astype(FULL)
    for other in [swap(back[d], "row", 2 * d) for d in (2, 1, 3)]:
        total = total + other.astype(FULL)
    terms = (terms + zero) + other_terms[0]
    terms = terms + swap(terms, "col", 2)
    terms = (terms + swap(terms, "col", 4)) + (swap(terms, "col", 8) + swap(terms, "col", 12))
    terms = terms + swap(terms, "col", 1)
    away = swap(total[nodes:].astype(HALF), "row", 1)
    total = total[:nodes] + away.astype(FULL)
    feature_grad = jnp.swapaxes(total.reshape(per, width, side), 1, 2).astype(HALF).reshape(nodes, width)
    return (activated, feature_grad, terms[:width], terms[width])


def solution(mesh):
    in_specs = (
        P(("col", "row"), None),
        P(),
        P(),
        P("row", "col", None, None, None),
        P("row", "col", None),
        P("row", "col", None),
        P("row", "col"),
        P(("row", "col"), None),
    )
    out_specs = (P(("row", "col"), None), P(("col", "row"), None), P(), P())
    return jax.shard_map(shards, mesh=mesh, in_specs=in_specs, out_specs=out_specs, check_vma=False)
```

```python
import functools

import jax
import jax.numpy as jnp
from jax import lax
from jax.experimental import pallas as pl
from jax.experimental.pallas import tpu as pltpu
from jax.sharding import PartitionSpec as P

HALF = jnp.bfloat16
FULL = jnp.float32


def swap(array, axis, distance):
    size = lax.axis_size(axis)
    return lax.ppermute(array, axis, [(j, j ^ distance) for j in range(size)])


def tile_kernel(chunk, num_pieces, num_totals, num_ready, flip, table_any, *refs):
    values_hbm = refs[0]
    pieces = refs[1 : 1 + num_pieces]
    outs = refs[1 + num_pieces + num_ready : -6]
    source, values, total, sems = refs[-6:-2]
    table_ref, table_sem = refs[-2:]
    num_chunks = values.shape[0] // chunk

    def copy(i):
        span = pl.ds(i * chunk, chunk)
        return pltpu.make_async_copy(values_hbm.at[span], values.at[span], sems.at[i])

    fetch = pltpu.make_async_copy(table_any, table_ref, table_sem)
    fetch.start()
    copy(0).start()
    first = 0
    for piece in pieces:
        tiles = piece.shape[0] // source.shape[1]
        source[pl.ds(first, tiles)] = piece[...].reshape((tiles,) + source.shape[1:])
        first += tiles
    fetch.wait()
    live_chunks = table_ref[values.shape[0]]
    for i in range(1, num_chunks):

        @pl.when(i < live_chunks)
        def _():
            copy(i).start()

    total[...] = jnp.zeros_like(total)

    def step(i, carry):
        copy(i).wait()
        products, targets = [], []
        for u in range(chunk):
            slot = i * chunk + u
            entry = table_ref[slot]
            picked = source[entry & 255]
            pair = (picked, values[slot]) if flip else (values[slot], picked)
            products.append(jnp.dot(*pair, preferred_element_type=FULL))
            targets.append(entry >> 8)
        for target, product in zip(targets, products):
            total[target] += product
        return carry

    lax.fori_loop(0, live_chunks, step, 0)
    first = 0
    for out in outs[:num_totals]:
        tiles = out.shape[0] // total.shape[1]
        out[...] = total[pl.ds(first, tiles)].astype(out.dtype).reshape(out.shape)
        first += tiles
    for out in outs[num_totals:]:
        out[...] = jnp.zeros_like(out)


def tile_sums(values, pieces, source_index, target_index, count, out_types, flip, zero_shape=None, ready=None):
    slots, side, _ = values.shape
    chunk = max(d for d in range(1, 65) if slots % d == 0)
    num_source = sum(piece.shape[0] for piece in pieces) // side
    num_out = sum(n for n, _ in out_types)
    width = pieces[0].shape[1]
    target_index = jnp.where(jnp.arange(slots, dtype=jnp.int32) < count, target_index, num_out)
    table = jnp.concatenate([source_index | (target_index << 8), jnp.maximum((count + chunk - 1) // chunk, 1)])
    vmem = pl.BlockSpec(memory_space=pltpu.VMEM)
    return pl.pallas_call(
        functools.partial(tile_kernel, chunk, len(pieces), len(out_types), int(ready is not None), flip),
        out_shape=[jax.ShapeDtypeStruct((n * side, width), kind) for n, kind in out_types]
        + ([jax.ShapeDtypeStruct(zero_shape, FULL)] if zero_shape else []),
        in_specs=[pl.BlockSpec(memory_space=pl.ANY), pl.BlockSpec(memory_space=pltpu.HBM)] + [vmem] * len(pieces)
        + [pl.BlockSpec(memory_space=pl.ANY)] * (ready is not None),
        out_specs=[vmem] * (len(out_types) + bool(zero_shape)),
        scratch_shapes=[
            pltpu.VMEM((num_source, side, width), HALF),
            pltpu.VMEM((slots, side, side), HALF),
            pltpu.VMEM((num_out + 1, side, width), FULL),
            pltpu.SemaphoreType.DMA((slots // chunk,)),
            pltpu.SMEM(table.shape, jnp.int32),
            pltpu.SemaphoreType.DMA,
        ],
        cost_estimate=pl.CostEstimate(
            flops=8 * slots * side * side * width, bytes_accessed=2 * slots * side * side, transcendentals=0
        ),
        compiler_params=pltpu.CompilerParams(vmem_limit_bytes=42 * 2**20),
    )(table, pltpu.with_memory_space_constraint(values, pltpu.HBM), *pieces, *([] if ready is None else [ready]))


def copy_kernel(array_ref, _, out_ref):
    out_ref[...] = array_ref[...]


def copy_after(array, event):
    return pl.pallas_call(
        copy_kernel,
        out_shape=jax.ShapeDtypeStruct(array.shape, array.dtype),
        in_specs=[pl.BlockSpec(memory_space=pltpu.VMEM), pl.BlockSpec(memory_space=pl.ANY)],
        out_specs=pl.BlockSpec(memory_space=pltpu.VMEM),
        compiler_params=pltpu.CompilerParams(vmem_limit_bytes=8 * 2**20),
    )(array, event)


def finish_kernel(total_ref, away_ref, terms_ref, other_ref, feature_ref, weight_ref, bias_ref):
    side = total_ref.shape[1]
    for first in range(0, feature_ref.shape[0], side):
        span = slice(first, first + side)
        tile = total_ref[span] + away_ref[span].astype(FULL)
        feature_ref[span] = tile.T.astype(feature_ref.dtype)
    rows = weight_ref.shape[0]
    weight_ref[...] = terms_ref[:rows] + other_ref[:rows]
    bias_ref[...] = terms_ref[rows : rows + 1] + other_ref[rows : rows + 1]


def after(array, event):
    return lax.optimization_barrier((array, event))[0]


def shards(features, weight, bias, tile_values, tile_rows, tile_cols, tile_count, upstream):
    side = tile_values.shape[3]
    width = features.shape[1]
    hidden = weight.shape[1]
    nodes = features.shape[0]
    per = nodes // side
    values = tile_values.reshape(tile_values.shape[2:])
    rows = tile_rows.reshape(-1)
    cols = tile_cols.reshape(-1)
    count = tile_count.reshape(1)
    my_row = lax.axis_index("row")
    my_col = lax.axis_index("col")
    row_owner = (rows // per) ^ my_col
    row_place = (row_owner % 2) * (lax.axis_size("col") // 2 * per) + (row_owner // 2) * per + rows % per
    col_place = ((cols // per) ^ my_row) * per + cols % per

    pair = jnp.concatenate([features, swap(features, "row", 1)], axis=0)
    pieces = [pair] + [swap(pair, "row", d) for d in (2, 4, 6)]
    up_away = swap(copy_after(upstream, pair), "col", 2)
    half_tiles = lax.axis_size("col") // 2 * per
    keep, send = tile_sums(
        values, pieces, col_place, row_place, count, [(half_tiles, FULL), (half_tiles, HALF)], False, ready=up_away
    )

    block = (keep + swap(send, "col", 1).astype(FULL)).astype(HALF).reshape(4, 2 * nodes, width)
    total = block[0].astype(FULL)
    for other in [swap(block[d], "col", 4 * d) for d in (2, 1, 3)]:
        total = total + other.astype(FULL)
    both = total.astype(HALF)
    both = (both.astype(FULL) + swap(jnp.concatenate([both[nodes:], both[:nodes]], axis=0), "col", 2).astype(FULL)).astype(HALF)
    up = jnp.concatenate([upstream, up_away], axis=0)
    pre = jnp.dot(both, weight, preferred_element_type=FULL) + bias
    activated = jax.nn.gelu(pre[:nodes], approximate=True).astype(HALF)
    _, pullback = jax.vjp(lambda v: jax.nn.gelu(v, approximate=True), pre)
    grad_both = pullback(up.astype(FULL))[0].astype(HALF)
    grad_tiles = grad_both.reshape(2 * per, side, hidden)
    pair = jnp.einsum("fh,tbh->tfb", weight, grad_tiles, preferred_element_type=FULL).astype(HALF)
    pair = pair.reshape(2 * per * width, side)
    grad_agg = pair
    s_half, grad_pre = both[:nodes], grad_both[:nodes]

    s_half, grad_pre = after((s_half, grad_pre), grad_agg)
    weight_term = jnp.dot(s_half.T, grad_pre, preferred_element_type=FULL)
    bias_term = jnp.sum(grad_pre.astype(FULL), axis=0)
    terms = jnp.concatenate([weight_term, jnp.broadcast_to(bias_term[None], (8, hidden))], axis=0)
    terms = (terms + swap(terms, "row", 2)) + (swap(terms, "row", 4) + swap(terms, "row", 6))
    near = [pair] + [swap(pair, "col", d) for d in (4, 8, 12)]
    far = [swap(piece, "col", 1) for piece in near]
    other_terms = [swap(terms, "row", 1)]
    back, zero = tile_sums(
        values, near + far, row_place, col_place, count, [(lax.axis_size("row") * per, HALF)], True, terms.shape
    )
    back = back.reshape(4, 2 * nodes, side)
    total = back[0].astype(FULL)
    for other in [swap(back[d], "row", 2 * d) for d in (2, 1, 3)]:
        total = total + other.astype(FULL)
    terms = (terms + zero) + other_terms[0]
    terms = terms + swap(terms, "col", 2)
    terms = terms + swap(terms, "col", 4)
    terms = terms + swap(terms, "col", 8)
    away = swap(total[nodes:].astype(HALF), "row", 1)
    feature_grad, weight_grad, bias_grad = pl.pallas_call(
        finish_kernel,
        out_shape=[
            jax.ShapeDtypeStruct((nodes, width), HALF),
            jax.ShapeDtypeStruct((width, hidden), FULL),
            jax.ShapeDtypeStruct((1, hidden), FULL),
        ],
        in_specs=[pl.BlockSpec(memory_space=pltpu.VMEM)] * 4,
        out_specs=[pl.BlockSpec(memory_space=pltpu.VMEM)] * 3,
        compiler_params=pltpu.CompilerParams(vmem_limit_bytes=8 * 2**20),
    )(total, away, terms, swap(terms, "col", 1))
    return (activated, feature_grad, weight_grad, bias_grad.reshape(hidden))


def solution(mesh):
    in_specs = (
        P(("col", "row"), None),
        P(),
        P(),
        P("row", "col", None, None, None),
        P("row", "col", None),
        P("row", "col", None),
        P("row", "col"),
        P(("row", "col"), None),
    )
    out_specs = (P(("row", "col"), None), P(("col", "row"), None), P(), P())
    return jax.shard_map(shards, mesh=mesh, in_specs=in_specs, out_specs=out_specs, check_vma=False)
```

```python
import functools

import jax
import jax.numpy as jnp
from jax import lax
from jax.experimental import pallas as pl
from jax.experimental.pallas import tpu as pltpu
from jax.sharding import PartitionSpec as P

HALF = jnp.bfloat16
FULL = jnp.float32


def swap(array, axis, distance):
    size = lax.axis_size(axis)
    return lax.ppermute(array, axis, [(j, j ^ distance) for j in range(size)])


def tile_kernel(chunk, num_pieces, num_totals, num_ready, flip, table_any, *refs):
    values_hbm = refs[0]
    pieces = refs[1 : 1 + num_pieces]
    outs = refs[1 + num_pieces + num_ready : -6]
    source, values, total, sems = refs[-6:-2]
    table_ref, table_sem = refs[-2:]
    num_chunks = values.shape[0] // chunk

    def copy(i):
        span = pl.ds(i * chunk, chunk)
        return pltpu.make_async_copy(values_hbm.at[span], values.at[span], sems.at[i])

    fetch = pltpu.make_async_copy(table_any, table_ref, table_sem)
    fetch.start()
    copy(0).start()
    first = 0
    for piece in pieces:
        tiles = piece.shape[0] // source.shape[1]
        source[pl.ds(first, tiles)] = piece[...].reshape((tiles,) + source.shape[1:])
        first += tiles
    fetch.wait()
    live_chunks = table_ref[values.shape[0]]
    for i in range(1, num_chunks):

        @pl.when(i < live_chunks)
        def _():
            copy(i).start()

    total[...] = jnp.zeros_like(total)

    def step(i, carry):
        copy(i).wait()
        products, targets = [], []
        for u in range(chunk):
            slot = i * chunk + u
            entry = table_ref[slot]
            picked = source[entry & 255]
            pair = (picked, values[slot]) if flip else (values[slot], picked)
            products.append(jnp.dot(*pair, preferred_element_type=FULL))
            targets.append(entry >> 8)
        for target, product in zip(targets, products):
            total[target] += product
        return carry

    lax.fori_loop(0, live_chunks, step, 0)
    first = 0
    for out in outs[:num_totals]:
        tiles = out.shape[0] // total.shape[1]
        out[...] = total[pl.ds(first, tiles)].astype(out.dtype).reshape(out.shape)
        first += tiles
    for out in outs[num_totals:]:
        out[...] = jnp.zeros_like(out)


def tile_sums(values, pieces, source_index, target_index, count, out_types, flip, zero_shape=None, ready=None):
    slots, side, _ = values.shape
    chunk = max(d for d in range(1, 89) if slots % d == 0)
    num_source = sum(piece.shape[0] for piece in pieces) // side
    num_out = sum(n for n, _ in out_types)
    width = pieces[0].shape[1]
    target_index = jnp.where(jnp.arange(slots, dtype=jnp.int32) < count, target_index, num_out)
    table = jnp.concatenate([source_index | (target_index << 8), jnp.maximum((count + chunk - 1) // chunk, 1)])
    vmem = pl.BlockSpec(memory_space=pltpu.VMEM)
    return pl.pallas_call(
        functools.partial(tile_kernel, chunk, len(pieces), len(out_types), int(ready is not None), flip),
        out_shape=[jax.ShapeDtypeStruct((n * side, width), kind) for n, kind in out_types]
        + ([jax.ShapeDtypeStruct(zero_shape, FULL)] if zero_shape else []),
        in_specs=[pl.BlockSpec(memory_space=pl.ANY), pl.BlockSpec(memory_space=pltpu.HBM)] + [vmem] * len(pieces)
        + [pl.BlockSpec(memory_space=pl.ANY)] * (ready is not None),
        out_specs=[vmem] * (len(out_types) + bool(zero_shape)),
        scratch_shapes=[
            pltpu.VMEM((num_source, side, width), HALF),
            pltpu.VMEM((slots, side, side), HALF),
            pltpu.VMEM((num_out + 1, side, width), FULL),
            pltpu.SemaphoreType.DMA((slots // chunk,)),
            pltpu.SMEM(table.shape, jnp.int32),
            pltpu.SemaphoreType.DMA,
        ],
        cost_estimate=pl.CostEstimate(
            flops=8 * slots * side * side * width, bytes_accessed=2 * slots * side * side, transcendentals=0
        ),
        compiler_params=pltpu.CompilerParams(vmem_limit_bytes=42 * 2**20),
    )(table, pltpu.with_memory_space_constraint(values, pltpu.HBM), *pieces, *([] if ready is None else [ready]))


def copy_kernel(array_ref, _, out_ref):
    out_ref[...] = array_ref[...]


def copy_after(array, event):
    return pl.pallas_call(
        copy_kernel,
        out_shape=jax.ShapeDtypeStruct(array.shape, array.dtype),
        in_specs=[pl.BlockSpec(memory_space=pltpu.VMEM), pl.BlockSpec(memory_space=pl.ANY)],
        out_specs=pl.BlockSpec(memory_space=pltpu.VMEM),
        compiler_params=pltpu.CompilerParams(vmem_limit_bytes=8 * 2**20),
    )(array, event)


def finish_kernel(total_ref, away_ref, terms_ref, other_ref, feature_ref, weight_ref, bias_ref):
    side = total_ref.shape[1]
    for first in range(0, feature_ref.shape[0], side):
        span = slice(first, first + side)
        tile = total_ref[span] + away_ref[span].astype(FULL)
        feature_ref[span] = tile.T.astype(feature_ref.dtype)
    rows = weight_ref.shape[0]
    weight_ref[...] = terms_ref[:rows] + other_ref[:rows]
    bias_ref[...] = terms_ref[rows : rows + 1] + other_ref[rows : rows + 1]


def after(array, event):
    return lax.optimization_barrier((array, event))[0]


def shards(features, weight, bias, tile_values, tile_rows, tile_cols, tile_count, upstream):
    side = tile_values.shape[3]
    width = features.shape[1]
    hidden = weight.shape[1]
    nodes = features.shape[0]
    per = nodes // side
    values = tile_values.reshape(tile_values.shape[2:])
    rows = tile_rows.reshape(-1)
    cols = tile_cols.reshape(-1)
    count = tile_count.reshape(1)
    my_row = lax.axis_index("row")
    my_col = lax.axis_index("col")
    row_owner = (rows // per) ^ my_col
    row_place = (row_owner % 2) * (lax.axis_size("col") // 2 * per) + (row_owner // 2) * per + rows % per
    col_place = ((cols // per) ^ my_row) * per + cols % per

    pair = jnp.concatenate([features, swap(features, "row", 1)], axis=0)
    pieces = [pair] + [swap(pair, "row", d) for d in (2, 4, 6)]
    up_away = swap(copy_after(upstream, pair), "col", 2)
    half_tiles = lax.axis_size("col") // 2 * per
    keep, send = tile_sums(
        values, pieces, col_place, row_place, count, [(half_tiles, FULL), (half_tiles, HALF)], False, ready=up_away
    )

    block = (keep + swap(send, "col", 1).astype(FULL)).astype(HALF).reshape(4, 2 * nodes, width)
    total = block[0].astype(FULL)
    for other in [swap(block[d], "col", 4 * d) for d in (2, 1, 3)]:
        total = total + other.astype(FULL)
    both = total.astype(HALF)
    both = (both.astype(FULL) + swap(jnp.concatenate([both[nodes:], both[:nodes]], axis=0), "col", 2).astype(FULL)).astype(HALF)
    up = jnp.concatenate([upstream, up_away], axis=0)
    pre = jnp.dot(both, weight, preferred_element_type=FULL) + bias
    activated = jax.nn.gelu(pre[:nodes], approximate=True).astype(HALF)
    _, pullback = jax.vjp(lambda v: jax.nn.gelu(v, approximate=True), pre)
    grad_both = pullback(up.astype(FULL))[0].astype(HALF)
    grad_tiles = grad_both.reshape(2 * per, side, hidden)
    pair = jnp.einsum("fh,tbh->tfb", weight, grad_tiles, preferred_element_type=FULL).astype(HALF)
    pair = pair.reshape(2 * per * width, side)
    grad_agg = pair
    s_half, grad_pre = both[:nodes], grad_both[:nodes]

    s_half, grad_pre = after((s_half, grad_pre), grad_agg)
    weight_term = jnp.dot(s_half.T, grad_pre, preferred_element_type=FULL)
    bias_term = jnp.sum(grad_pre.astype(FULL), axis=0)
    terms = jnp.concatenate([weight_term, jnp.broadcast_to(bias_term[None], (8, hidden))], axis=0)
    terms = (terms + swap(terms, "row", 2)) + (swap(terms, "row", 4) + swap(terms, "row", 6))
    near = [pair] + [swap(pair, "col", d) for d in (4, 8, 12)]
    far = [swap(piece, "col", 1) for piece in near]
    other_terms = [swap(terms, "row", 1)]
    back, zero = tile_sums(
        values, near + far, row_place, col_place, count, [(lax.axis_size("row") * per, HALF)], True, terms.shape
    )
    back = back.reshape(4, 2 * nodes, side)
    total = back[0].astype(FULL)
    for other in [swap(back[d], "row", 2 * d) for d in (2, 1, 3)]:
        total = total + other.astype(FULL)
    terms = (terms + zero) + other_terms[0]
    terms = terms + swap(terms, "col", 2)
    terms = terms + swap(terms, "col", 4)
    terms = terms + swap(terms, "col", 8)
    away = swap(total[nodes:].astype(HALF), "row", 1)
    feature_grad, weight_grad, bias_grad = pl.pallas_call(
        finish_kernel,
        out_shape=[
            jax.ShapeDtypeStruct((nodes, width), HALF),
            jax.ShapeDtypeStruct((width, hidden), FULL),
            jax.ShapeDtypeStruct((1, hidden), FULL),
        ],
        in_specs=[pl.BlockSpec(memory_space=pltpu.VMEM)] * 4,
        out_specs=[pl.BlockSpec(memory_space=pltpu.VMEM)] * 3,
        compiler_params=pltpu.CompilerParams(vmem_limit_bytes=8 * 2**20),
    )(total, away, terms, swap(terms, "col", 1))
    return (activated, feature_grad, weight_grad, bias_grad.reshape(hidden))


def solution(mesh):
    in_specs = (
        P(("col", "row"), None),
        P(),
        P(),
        P("row", "col", None, None, None),
        P("row", "col", None),
        P("row", "col", None),
        P("row", "col"),
        P(("row", "col"), None),
    )
    out_specs = (P(("row", "col"), None), P(("col", "row"), None), P(), P())
    return jax.shard_map(shards, mesh=mesh, in_specs=in_specs, out_specs=out_specs, check_vma=False)
```
